512 devices in a mesh: row: 4 (over x), col: 16 (over z), depth: 8 (over y, core).
Axes of the slice: x: 4, y: 4, z: 16, core: 2. Of those that a mesh axis runs over, the one named last changes fastest.
Arguments:
- tokens: bfloat16 [512, 8192], P(('row', 'depth'), 'col'), may hold values from -6 to 6
- cotangent: bfloat16 [512, 8192], P(('row', 'depth'), 'col'), may hold values from -6 to 6
- gate_weight: bfloat16 [8192, 14336], P('col', ('row', 'depth')), may hold values from -0.0625 to 0.0625
- up_weight: bfloat16 [8192, 14336], P('col', ('row', 'depth')), may hold values from -0.0625 to 0.0625
- down_weight: bfloat16 [14336, 8192], P(('row', 'depth'), 'col'), may hold values from -0.046875 to 0.046875
Outputs:
- layer_out: bfloat16 [512, 8192], P(('row', 'depth'), 'col')
- tokens_grad: bfloat16 [512, 8192], P(('row', 'depth'), 'col')
- gate_grad: bfloat16 [8192, 14336], P('col', ('row', 'depth'))
- up_grad: bfloat16 [8192, 14336], P('col', ('row', 'depth'))
- down_grad: bfloat16 [14336, 8192], P(('row', 'depth'), 'col')
The draws below stay inside these ranges and needn't reach their ends.
All inputs are finite; a program needn't handle non-finite values.
Results may differ from the reference program's by a relative error of at most 0.0049.
Values may be sent and summed in bfloat16 or wider, within the bound.
No kernel may reach another device: no remote copies, remote signals or barrier semaphores. Data moves between devices by JAX's collectives and lax.ppermute only.
A program may use at most 64 MiB of HBM per device.

```python
import math
import jax
import jax.numpy as jnp

D = 8192
FF = 14336
TOKENS = 512


def block_levels(rng, shape, cuts, smallest, largest):
    factor_of = 1.0
    for axis_at, blocks in cuts:
        draws = jax.random.uniform(jax.random.fold_in(jax.random.fold_in(rng, 6), axis_at), (blocks,), jnp.float32, smallest / len(cuts), largest / len(cuts))
        factor_of = factor_of * jnp.repeat(jnp.exp(draws), shape[axis_at] // blocks).reshape((-1,) + (1,) * (len(shape) - 1 - axis_at))
    return factor_of


def bell_draw(key, shape, spread, reach, split=(), held_as=jnp.bfloat16):
    gain = block_levels(key, shape, split, -0.22, 0.18) if split else 1.0
    values = jax.random.normal(key, shape, jnp.float32) * spread * gain
    return jnp.minimum(jnp.maximum(values, -reach), reach).astype(held_as)


def setup_inputs(seed: int = 0) -> dict:
    key_list = jax.random.split(jax.random.key(seed), 6)
    tokens = bell_draw(key_list[0], (TOKENS, D), 1.0, 6.0, ((0, 32), (1, 16)))
    cotangent = bell_draw(key_list[1], (TOKENS, D), 1.0, 6.0, ((0, 32), (1, 16)))
    gate_weight = bell_draw(key_list[2], (D, FF), D ** -0.5, 0.0625, ((0, 16), (1, 32)))
    up_weight = bell_draw(key_list[3], (D, FF), D ** -0.5, 0.0625, ((0, 16), (1, 32)))
    down_weight = bell_draw(key_list[4], (FF, D), FF ** -0.5, 0.046875, ((0, 32), (1, 16)))
    return {"tokens": tokens, "cotangent": cotangent, "gate_weight": gate_weight, "up_weight": up_weight, "down_weight": down_weight}


def reference(tokens, cotangent, gate_weight, up_weight, down_weight):
    gate_sum = jnp.dot(tokens, gate_weight, preferred_element_type=jnp.float32)
    up_sum = jnp.dot(tokens, up_weight, preferred_element_type=jnp.float32)
    sigmoid_gate = jax.nn.sigmoid(gate_sum)
    hidden = (gate_sum * sigmoid_gate * up_sum).astype(jnp.bfloat16)
    layer_out = jnp.dot(hidden, down_weight, preferred_element_type=jnp.float32).astype(jnp.bfloat16)
    hidden_cot = jnp.dot(cotangent, down_weight.T, preferred_element_type=jnp.float32)
    grad_scale = 1.0 / math.sqrt(TOKENS)
    down_grad = (jnp.dot(hidden.T, cotangent, preferred_element_type=jnp.float32) * grad_scale).astype(jnp.bfloat16)
    gate_cot = (hidden_cot * up_sum * sigmoid_gate * (1.0 + gate_sum * (1.0 - sigmoid_gate))).astype(jnp.bfloat16)
    up_cot = (hidden_cot * gate_sum * sigmoid_gate).astype(jnp.bfloat16)
    gate_grad = (jnp.dot(tokens.T, gate_cot, preferred_element_type=jnp.float32) * grad_scale).astype(jnp.bfloat16)
    up_grad = (jnp.dot(tokens.T, up_cot, preferred_element_type=jnp.float32) * grad_scale).astype(jnp.bfloat16)
    back_sum = jnp.dot(gate_cot, gate_weight.T, preferred_element_type=jnp.float32)
    back_sum = back_sum + jnp.dot(up_cot, up_weight.T, preferred_element_type=jnp.float32)
    tokens_grad = back_sum.astype(jnp.bfloat16)
    return (layer_out, tokens_grad, gate_grad, up_grad, down_grad)
```

```python
import math

import jax
import jax.numpy as jnp
from jax import lax
from jax.experimental import pallas as pl
from jax.experimental.pallas import tpu as pltpu
from jax.sharding import PartitionSpec as P

BF = jnp.bfloat16
F32 = jnp.float32
GROUP = ("row", "depth")
NEAR = (0, -1, 1, 2)


def nt(left, right):
    return lax.dot_general(left, right, (((1,), (1,)), ((), ())), preferred_element_type=F32)


def nn(left, right):
    return lax.dot_general(left, right, (((1,), (0,)), ((), ())), preferred_element_type=F32)


def tn(left, right):
    return lax.dot_general(left, right, (((0,), (0,)), ((), ())), preferred_element_type=F32)


def call(body, out_shapes, n_scalar, n_array, scratch=()):
    return pl.pallas_call(
        body,
        out_shape=[jax.ShapeDtypeStruct(s, d) for s, d in out_shapes],
        in_specs=[pl.BlockSpec(memory_space=pltpu.SMEM)] * n_scalar
        + [pl.BlockSpec(memory_space=pltpu.VMEM)] * n_array,
        out_specs=[pl.BlockSpec(memory_space=pltpu.VMEM)] * len(out_shapes),
        scratch_shapes=list(scratch),
        compiler_params=pltpu.CompilerParams(vmem_limit_bytes=40 * 1024 * 1024),
    )


def partial_sums(index, gathered, gate_t, up_t, down, own, first, second, third, ordered, pair):
    ff = gate_t.shape[0]
    width = gate_t.shape[1]
    pair[0:ff, :] = gate_t[...]
    pair[ff : 2 * ff, :] = up_t[...]
    chunk = ordered.shape[0] // 16
    per = chunk // gathered.shape[1]
    for at in range(16):
        rows = gathered[pl.ds(index[at] * per, per)]
        ordered[at * chunk : (at + 1) * chunk, :] = rows.reshape(chunk, 2 * width)
    block = 4 * chunk
    for at, out in enumerate((own, first, second, third)):
        rows = ordered[at * block : (at + 1) * block, :]
        out[:, 0 : 2 * ff] = nt(rows[:, :width], pair[...]).astype(out.dtype)
        out[:, 2 * ff :] = nt(rows[:, width:], down[...]).astype(out.dtype)


def near_sum(place, own, first, second, third, keep, near, far, back):
    chunk = keep.shape[0]

    def total(at):
        rows = pl.ds(pl.multiple_of(place[at] * chunk, chunk), chunk)
        return own[rows, :] + (
            first[rows, :].astype(F32) + second[rows, :].astype(F32) + third[rows, :].astype(F32)
        )

    keep[...] = total(0)
    near[...] = total(1).astype(BF)
    far[...] = total(2).astype(BF)
    back[...] = total(3).astype(BF)


def swish(keep, near, far, back, out):
    ff = out.shape[1] // 3
    total = keep[...] + (near[...].astype(F32) + far[...].astype(F32) + back[...].astype(F32))
    gate_sum = total[:, :ff]
    up_sum = total[:, ff : 2 * ff]
    hidden_cot = total[:, 2 * ff :]
    sig = jax.nn.sigmoid(gate_sum)
    gate_cot = hidden_cot * up_sum * sig * (1.0 + gate_sum * (1.0 - sig))
    up_cot = hidden_cot * gate_sum * sig
    out[:, :ff] = gate_cot.astype(BF)
    out[:, ff : 2 * ff] = up_cot.astype(BF)
    out[:, 2 * ff :] = (gate_sum * sig * up_sum).astype(BF)


def outward(index, c0, c1, c2, c3, gate_t, up_t, down, out, pair):
    ff = gate_t.shape[0]
    width = gate_t.shape[1]
    pair[0:ff, :] = gate_t[...]
    pair[ff : 2 * ff, :] = up_t[...]
    chunk = out.shape[1]
    for at, c in enumerate((c0, c1, c2, c3)):
        layer = nn(c[:, 2 * ff :], down[...]).astype(BF)
        back = nn(c[:, : 2 * ff], pair[...]).astype(BF)
        for j in range(4):
            slot = index[at * 4 + j]
            out[slot, :, :width] = layer[j * chunk : (j + 1) * chunk, :]
            out[slot, :, width:] = back[j * chunk : (j + 1) * chunk, :]


def weight_grads(c0, c1, c2, c3, ordered, gate_g, up_g, down_g, allc):
    ff, width = gate_g.shape
    block = c0.shape[0]
    scale = 1.0 / math.sqrt(ordered.shape[0])
    for at, c in enumerate((c0, c1, c2, c3)):
        allc[at * block : (at + 1) * block, :] = c[...]
    both = tn(allc[:, : 2 * ff], ordered[:, :width]) * scale
    gate_g[...] = both[:ff, :].astype(BF)
    up_g[...] = both[ff:, :].astype(BF)
    down_g[...] = (tn(allc[:, 2 * ff :], ordered[:, width:]) * scale).astype(BF)


def shards(mesh, tokens, cotangent, gate_weight, up_weight, down_weight):
    cols, depth = mesh.shape["col"], mesh.shape["depth"]
    ranks = mesh.shape["row"] * depth
    ff, width = down_weight.shape
    rows = tokens.shape[0]
    total = rows * ranks
    chunk = total // cols
    block = 4 * chunk

    def shift(x, step):
        pairs = []
        for z in range(cols):
            for d in range(depth):
                to = (z + (step if d % 2 == 0 else -step)) % cols
                pairs.append((z * depth + d, to * depth + d))
        return lax.ppermute(x, ("col", "depth"), pairs)

    z = lax.axis_index("col")
    sign = 1 - 2 * (lax.axis_index("depth") % 2)
    four = jnp.arange(4, dtype=jnp.int32)
    classes = (z - sign * jnp.array(NEAR, jnp.int32) + 16) % 4
    index = (classes[:, None] + 4 * four[None, :]).reshape(16).astype(jnp.int32)
    place = ((z // 4 + sign * four + 4) % 4).astype(jnp.int32)

    mine = jnp.concatenate([tokens, cotangent], axis=1)
    gathered = lax.all_to_all(
        jnp.broadcast_to(mine[None], (ranks, rows, 2 * width)), GROUP, 0, 0, tiled=True
    )
    gate_t, up_t = gate_weight.T, up_weight.T
    wide = 3 * ff
    own, first, second, third, ordered = call(
        partial_sums,
        [((block, wide), F32)] + [((block, wide), BF)] * 3 + [((total, 2 * width), BF)],
        1,
        4,
        [pltpu.VMEM((2 * ff, width), BF)],
    )(index, gathered, gate_t, up_t, down_weight)
    third = shift(third, -NEAR[3])
    first = shift(first, -NEAR[1])
    second = shift(second, -NEAR[2])
    keep, near, far, back = call(
        near_sum, [((chunk, wide), F32)] + [((chunk, wide), BF)] * 3, 1, 4
    )(place, own, first, second, third)
    far = shift(far, 8)
    near = shift(near, 4)
    back = shift(back, -4)
    (act,) = call(swish, [((chunk, wide), BF)], 0, 4)(keep, near, far, back)
    strided = [[i + 4 * j for j in range(4)] for i in range(4)]
    c0 = lax.all_gather(act, "col", axis=0, tiled=True, axis_index_groups=strided)
    c3 = shift(c0, NEAR[3])
    c1 = shift(c0, NEAR[1])
    c2 = shift(c0, NEAR[2])
    (out,) = call(
        outward,
        [((16, chunk, 2 * width), BF)],
        1,
        7,
        [pltpu.VMEM((2 * ff, width), BF)],
    )(index, c0, c1, c2, c3, gate_t, up_t, down_weight)
    parts = lax.all_to_all(out.reshape(ranks, rows, 2 * width), GROUP, 0, 0, tiled=True)
    summed = jnp.sum(parts.astype(F32), axis=0).astype(BF)
    gate_g, up_g, down_g = call(
        weight_grads, [((ff, width), BF)] * 3, 0, 5, [pltpu.VMEM((total, wide), BF)]
    )(c0, c1, c2, c3, ordered)
    return (summed[:, :width], summed[:, width:], gate_g.T, up_g.T, down_g)


def solution(mesh):
    tok = P(GROUP, "col")
    wide = P("col", GROUP)

    def run(*args):
        return shards(mesh, *args)

    return jax.shard_map(
        run,
        mesh=mesh,
        in_specs=(tok, tok, wide, wide, tok),
        out_specs=(tok, tok, wide, wide, tok),
        check_vma=False,
    )
```

```python
import math

import jax
import jax.numpy as jnp
from jax import lax
from jax.experimental import pallas as pl
from jax.experimental.pallas import tpu as pltpu
from jax.sharding import PartitionSpec as P

BF = jnp.bfloat16
F32 = jnp.float32
GROUP = ("row", "depth")
NEAR = (0, -1, 1, 2)


def nt(left, right):
    return lax.dot_general(left, right, (((1,), (1,)), ((), ())), preferred_element_type=F32)


def nn(left, right):
    return lax.dot_general(left, right, (((1,), (0,)), ((), ())), preferred_element_type=F32)


def tn(left, right):
    return lax.dot_general(left, right, (((0,), (0,)), ((), ())), preferred_element_type=F32)


def call(body, out_shapes, n_scalar, n_array, scratch=(), mib=8):
    return pl.pallas_call(
        body,
        out_shape=[jax.ShapeDtypeStruct(s, d) for s, d in out_shapes],
        in_specs=[pl.BlockSpec(memory_space=pltpu.SMEM)] * n_scalar
        + [pl.BlockSpec(memory_space=pltpu.VMEM)] * n_array,
        out_specs=[pl.BlockSpec(memory_space=pltpu.VMEM)] * len(out_shapes),
        scratch_shapes=list(scratch),
        compiler_params=pltpu.CompilerParams(vmem_limit_bytes=mib * 1024 * 1024),
    )


def coded(x):
    return (x * jnp.abs(x)).astype(BF)


def decoded(x):
    wide = x.astype(F32)
    root = jnp.sqrt(jnp.abs(wide))
    return jnp.where(wide < 0, -root, root)


def spread(tokens, cotangent, out):
    width = tokens.shape[1]
    both = jnp.concatenate([tokens[...], cotangent[...]], axis=1)
    for at in range(out.shape[0]):
        out[at] = both


def partial_sums(index, gathered, pair, down, third, first, second, own, ordered):
    width = pair.shape[1]
    both = pair.shape[0]
    chunk = ordered.shape[0] // 16
    per = chunk // gathered.shape[1]
    block = 4 * chunk
    for at, out in ((3, third), (1, first), (2, second), (0, own)):
        for j in range(4):
            slot = at * 4 + j
            rows = gathered[pl.ds(index[slot] * per, per)]
            ordered[slot * chunk : (slot + 1) * chunk, :] = rows.reshape(chunk, 2 * width)
        rows = ordered[at * block : (at + 1) * block, :]
        gate_up = nt(rows[:, :width], pair[...])
        cot = nt(rows[:, width:], down[...])
        out[:, 0:both] = gate_up if at == 0 else coded(gate_up)
        out[:, both:] = cot if at == 0 else coded(cot)


def near_sum(place, own, first, second, third, far, near, back, keep):
    chunk = keep.shape[0]

    def total(at):
        rows = pl.ds(pl.multiple_of(place[at] * chunk, chunk), chunk)
        return own[rows, :] + (decoded(first[rows, :]) + decoded(second[rows, :]) + decoded(third[rows, :]))

    far[...] = coded(total(2))
    near[...] = coded(total(1))
    back[...] = coded(total(3))
    keep[...] = total(0)


def swish(keep, near, far, back, out):
    ff = out.shape[1] // 3
    total = keep[...] + (decoded(near[...]) + decoded(far[...]) + decoded(back[...]))
    gate_sum = total[:, :ff]
    up_sum = total[:, ff : 2 * ff]
    hidden_cot = total[:, 2 * ff :]
    sig = jax.nn.sigmoid(gate_sum)
    gate_cot = hidden_cot * up_sum * sig * (1.0 + gate_sum * (1.0 - sig))
    up_cot = hidden_cot * gate_sum * sig
    out[:, :ff] = gate_cot.astype(BF)
    out[:, ff : 2 * ff] = up_cot.astype(BF)
    out[:, 2 * ff :] = (gate_sum * sig * up_sum).astype(BF)


def outward_rows(c, pair, down):
    both = pair.shape[0]
    return nn(c[:, both:], down[...]).astype(BF), nn(c[:, :both], pair[...]).astype(BF)


def outward_own(c0, pair, down, out):
    width = pair.shape[1]
    layer, back = outward_rows(c0, pair, down)
    out[:, :width] = layer
    out[:, width:] = back


def outward(index, own, c1, c2, c3, pair, down, out):
    width = pair.shape[1]
    chunk = out.shape[1]
    for j in range(4):
        out[index[j]] = own[j * chunk : (j + 1) * chunk, :]
    for at, c in ((1, c1), (2, c2), (3, c3)):
        layer, back = outward_rows(c, pair, down)
        for j in range(4):
            slot = index[at * 4 + j]
            out[slot, :, :width] = layer[j * chunk : (j + 1) * chunk, :]
            out[slot, :, width:] = back[j * chunk : (j + 1) * chunk, :]


def weight_grads(c0, c1, c2, c3, ordered, gate_g, up_g, down_g, allc):
    ff, width = gate_g.shape
    block = c0.shape[0]
    scale = 1.0 / math.sqrt(ordered.shape[0])
    for at, c in enumerate((c0, c1, c2, c3)):
        allc[at * block : (at + 1) * block, :] = c[...]
    both = tn(allc[:, : 2 * ff], ordered[:, :width]) * scale
    gate_g[...] = both[:ff, :].astype(BF)
    up_g[...] = both[ff:, :].astype(BF)
    down_g[...] = (tn(allc[:, 2 * ff :], ordered[:, width:]) * scale).astype(BF)


def last_sum(parts, layer_out, tokens_grad):
    width = layer_out.shape[1]
    total = parts[0].astype(F32)
    for at in range(1, parts.shape[0]):
        total = total + parts[at].astype(F32)
    layer_out[...] = total[:, :width].astype(BF)
    tokens_grad[...] = total[:, width:].astype(BF)


def shards(mesh, tokens, cotangent, gate_weight, up_weight, down_weight):
    cols, depth = mesh.shape["col"], mesh.shape["depth"]
    ranks = mesh.shape["row"] * depth
    ff, width = down_weight.shape
    rows = tokens.shape[0]
    total = rows * ranks
    chunk = total // cols
    block = 4 * chunk
    wide = 3 * ff

    def shift(x, step):
        pairs = []
        for z in range(cols):
            for d in range(depth):
                to = (z + (step if d % 2 == 0 else -step)) % cols
                pairs.append((z * depth + d, to * depth + d))
        return lax.ppermute(x, ("col", "depth"), pairs)

    z = lax.axis_index("col")
    sign = 1 - 2 * (lax.axis_index("depth") % 2)
    four = jnp.arange(4, dtype=jnp.int32)
    classes = (z - sign * jnp.array(NEAR, jnp.int32) + 16) % 4
    index = (classes[:, None] + 4 * four[None, :]).reshape(16).astype(jnp.int32)
    place = ((z // 4 + sign * four + 4) % 4).astype(jnp.int32)

    (mine,) = call(spread, [((ranks, rows, 2 * width), BF)], 0, 2)(tokens, cotangent)
    gathered = lax.all_to_all(mine, GROUP, 0, 0, tiled=True)
    pair = jnp.concatenate([gate_weight.T, up_weight.T], axis=0)
    third, first, second, own, ordered = call(
        partial_sums,
        [((block, wide), BF)] * 3 + [((block, wide), F32), ((total, 2 * width), BF)],
        1,
        3,
        mib=12,
    )(index, gathered, pair, down_weight)
    third = shift(third, -NEAR[3])
    first = shift(first, -NEAR[1])
    second = shift(second, -NEAR[2])
    far, near, back, keep = call(
        near_sum, [((chunk, wide), BF)] * 3 + [((chunk, wide), F32)], 1, 4
    )(place, own, first, second, third)
    far = shift(far, 8)
    near = shift(near, 4)
    back = shift(back, -4)
    (act,) = call(swish, [((chunk, wide), BF)], 0, 4)(keep, near, far, back)
    strided = [[i + 4 * j for j in range(4)] for i in range(4)]
    c0 = lax.all_gather(act, "col", axis=0, tiled=True, axis_index_groups=strided)
    c3 = shift(c0, NEAR[3])
    c1 = shift(c0, NEAR[1])
    c2 = shift(c0, NEAR[2])
    (own_out,) = call(outward_own, [((block, 2 * width), BF)], 0, 3)(c0, pair, down_weight)
    (out,) = call(outward, [((16, chunk, 2 * width), BF)], 1, 6)(
        index, own_out, c1, c2, c3, pair, down_weight
    )
    parts = lax.all_to_all(out.reshape(ranks, rows, 2 * width), GROUP, 0, 0, tiled=True)
    layer_out, tokens_grad = call(last_sum, [((rows, width), BF)] * 2, 0, 1)(parts)
    gate_g, up_g, down_g = call(
        weight_grads, [((ff, width), BF)] * 3, 0, 5, [pltpu.VMEM((total, wide), BF)], mib=12
    )(c0, c1, c2, c3, ordered)
    return (layer_out, tokens_grad, gate_g.T, up_g.T, down_g)


def solution(mesh):
    tok = P(GROUP, "col")
    wide = P("col", GROUP)

    def run(*args):
        return shards(mesh, *args)

    return jax.shard_map(
        run,
        mesh=mesh,
        in_specs=(tok, tok, wide, wide, tok),
        out_specs=(tok, tok, wide, wide, tok),
        check_vma=False,
    )
```

```python
import functools
import math

import jax
import jax.numpy as jnp
from jax import lax
from jax.experimental import pallas as pl
from jax.experimental.pallas import tpu as pltpu
from jax.sharding import PartitionSpec as P

BF = jnp.bfloat16
F32 = jnp.float32
GROUP = ("row", "depth")
NEAR = (0, -1, 1, 2)


def nt(left, right):
    return lax.dot_general(left, right, (((1,), (1,)), ((), ())), preferred_element_type=F32)


def nn(left, right):
    return lax.dot_general(left, right, (((1,), (0,)), ((), ())), preferred_element_type=F32)


def tn(left, right):
    return lax.dot_general(left, right, (((0,), (0,)), ((), ())), preferred_element_type=F32)


def call(body, out_shapes, n_scalar, n_array, scratch=(), mib=8, outside=(), outside_out=()):
    def place(at, away):
        return pl.BlockSpec(memory_space=pl.ANY if at in away else pltpu.VMEM)

    return pl.pallas_call(
        body,
        out_shape=[jax.ShapeDtypeStruct(s, d) for s, d in out_shapes],
        in_specs=[pl.BlockSpec(memory_space=pltpu.SMEM)] * n_scalar
        + [place(at, outside) for at in range(n_array)],
        out_specs=[place(at, outside_out) for at in range(len(out_shapes))],
        scratch_shapes=list(scratch),
        compiler_params=pltpu.CompilerParams(vmem_limit_bytes=mib * 1024 * 1024),
    )


def coded(x):
    return (x * jnp.abs(x)).astype(BF)


def decoded(x):
    wide = x.astype(F32)
    root = jnp.sqrt(jnp.abs(wide))
    return jnp.where(wide < 0, -root, root)


def spread(tokens, cotangent, out, both, sems):
    width = tokens.shape[1]
    left = pltpu.make_async_copy(tokens, both.at[:, :width], sems.at[0])
    right = pltpu.make_async_copy(cotangent, both.at[:, width:], sems.at[1])
    left.start()
    right.start()
    left.wait()
    right.wait()
    for at in range(out.shape[0]):
        out[at] = both[...]


def partial_sums(index, mine, other, pair, down, third, first, second, own, kept, ordered, sems):
    width = pair.shape[1]
    both = pair.shape[0]
    rows = mine.shape[1]
    chunk = 2 * rows
    block = 4 * chunk
    copies = []
    for at, out in ((3, third), (1, first), (2, second), (0, own)):
        for j in range(4):
            slot = at * 4 + j
            ordered[slot * chunk : slot * chunk + rows, :] = mine[index[slot]]
            ordered[slot * chunk + rows : (slot + 1) * chunk, :] = other[index[slot]]
        here = pl.ds(at * block, block)
        copies.append(pltpu.make_async_copy(ordered.at[here], kept.at[here], sems.at[at]))
        copies[-1].start()
        block_rows = ordered[at * block : (at + 1) * block, :]
        gate_up = nt(block_rows[:, :width], pair[...])
        cot = nt(block_rows[:, width:], down[...])
        out[:, 0:both] = gate_up if at == 0 else coded(gate_up)
        out[:, both:] = cot if at == 0 else coded(cot)
    for copy in copies:
        copy.wait()


def near_sum(place, own, third, first, second, far, near, back, keep):
    chunk = keep.shape[0]

    def total(at):
        rows = pl.ds(pl.multiple_of(place[at] * chunk, chunk), chunk)
        return own[rows, :] + (decoded(first[rows, :]) + decoded(second[rows, :]) + decoded(third[rows, :]))

    far[...] = coded(total(2))
    near[...] = coded(total(1))
    back[...] = coded(total(3))
    keep[...] = total(0)


def swish(keep, far, near, back, out):
    ff = out.shape[1] // 3
    total = keep[...] + (decoded(near[...]) + decoded(far[...]) + decoded(back[...]))
    gate_sum = total[:, :ff]
    up_sum = total[:, ff : 2 * ff]
    hidden_cot = total[:, 2 * ff :]
    sig = jax.nn.sigmoid(gate_sum)
    gate_cot = hidden_cot * up_sum * sig * (1.0 + gate_sum * (1.0 - sig))
    up_cot = hidden_cot * gate_sum * sig
    out[:, :ff] = gate_cot.astype(BF)
    out[:, ff : 2 * ff] = up_cot.astype(BF)
    out[:, 2 * ff :] = (gate_sum * sig * up_sum).astype(BF)


def outward(half, index, c3, c1, c2, c0, pair, down, out, picked):
    width = pair.shape[1]
    both = pair.shape[0]
    rows = out.shape[1]
    for at, c in ((3, c3), (1, c1), (2, c2), (0, c0)):
        for j in range(4):
            slot = at * 4 + j
            first = j * 2 * rows + half * rows
            picked[slot * rows : (slot + 1) * rows, :] = c[first : first + rows, :]
    layer = nn(picked[:, both:], down[...]).astype(out.dtype)
    back = nn(picked[:, :both], pair[...]).astype(out.dtype)
    for slot in range(16):
        out[index[slot], :, :width] = layer[slot * rows : (slot + 1) * rows, :]
        out[index[slot], :, width:] = back[slot * rows : (slot + 1) * rows, :]


def core_sum(keep, arrived, out):
    out[...] = (keep[...] + arrived[...].astype(F32)).astype(BF)


def weight_grads(c0, c1, c2, c3, ordered, gate_g, up_g, down_g, allc):
    ff, width = gate_g.shape
    block = c0.shape[0]
    scale = 1.0 / math.sqrt(ordered.shape[0])
    for at, c in enumerate((c0, c1, c2, c3)):
        allc[at * block : (at + 1) * block, :] = c[...]
    both = tn(allc[:, : 2 * ff], ordered[:, :width]) * scale
    gate_g[...] = both[:ff, :].astype(BF)
    up_g[...] = both[ff:, :].astype(BF)
    down_g[...] = (tn(allc[:, 2 * ff :], ordered[:, width:]) * scale).astype(BF)


def last_sum(parts, layer_out, tokens_grad):
    width = layer_out.shape[1]
    total = parts[0].astype(F32)
    for at in range(1, parts.shape[0]):
        total = total + parts[at].astype(F32)
    layer_out[...] = total[:, :width].astype(BF)
    tokens_grad[...] = total[:, width:].astype(BF)


def shards(mesh, tokens, cotangent, gate_weight, up_weight, down_weight):
    cols, depth = mesh.shape["col"], mesh.shape["depth"]
    ranks = mesh.shape["row"] * depth
    ff, width = down_weight.shape
    rows = tokens.shape[0]
    total = rows * ranks
    chunk = total // cols
    block = 4 * chunk
    wide = 3 * ff

    def shift(x, step):
        pairs = []
        for z in range(cols):
            for d in range(depth):
                to = (z + (step if d % 2 == 0 else -step)) % cols
                pairs.append((z * depth + d, to * depth + d))
        return lax.ppermute(x, ("col", "depth"), pairs)

    z = lax.axis_index("col")
    sign = 1 - 2 * (lax.axis_index("depth") % 2)
    four = jnp.arange(4, dtype=jnp.int32)
    classes = (z - sign * jnp.array(NEAR, jnp.int32) + 16) % 4
    index = (classes[:, None] + 4 * four[None, :]).reshape(16).astype(jnp.int32)
    place = ((z // 4 + sign * four + 4) % 4).astype(jnp.int32)

    cores = 2
    chips = ranks // cores
    same_core = [[c + cores * a for a in range(chips)] for c in range(cores)]

    def swap(x):
        return lax.ppermute(x, "depth", [(d, d ^ 1) for d in range(depth)])

    def exchange(x):
        return lax.all_to_all(x, GROUP, 0, 0, tiled=True, axis_index_groups=same_core)

    (sent,) = call(
        spread,
        [((chips, rows, 2 * width), BF)],
        0,
        2,
        [pltpu.VMEM((rows, 2 * width), BF), pltpu.SemaphoreType.DMA((2,))],
        outside=(0, 1),
    )(tokens, cotangent)
    mine = exchange(sent)
    other = swap(mine)
    pair = jnp.concatenate([gate_weight.T, up_weight.T], axis=0)
    third, first, second, own, ordered = call(
        partial_sums,
        [((block, wide), BF)] * 3 + [((block, wide), F32), ((total, 2 * width), BF)],
        1,
        4,
        [pltpu.VMEM((total, 2 * width), BF), pltpu.SemaphoreType.DMA((4,))],
        mib=12,
        outside_out=(4,),
    )(index, mine, other, pair, down_weight)
    third = shift(third, -NEAR[3])
    first = shift(first, -NEAR[1])
    second = shift(second, -NEAR[2])
    far, near, back, keep = call(
        near_sum, [((chunk, wide), BF)] * 3 + [((chunk, wide), F32)], 1, 4
    )(place, own, third, first, second)
    far = shift(far, 8)
    near = shift(near, 4)
    back = shift(back, -4)
    (act,) = call(swish, [((chunk, wide), BF)], 0, 4)(keep, far, near, back)
    strided = [[i + 4 * j for j in range(4)] for i in range(4)]
    c0 = lax.all_gather(act, "col", axis=0, tiled=True, axis_index_groups=strided)
    c3 = shift(c0, NEAR[3])
    c1 = shift(c0, NEAR[1])
    c2 = shift(c0, NEAR[2])
    def half_out(half, dtype):
        return call(
            functools.partial(outward, half),
            [((chips, rows, 2 * width), dtype)],
            1,
            6,
            [pltpu.VMEM((total // cores, wide), BF)],
        )(index, c3, c1, c2, c0, pair, down_weight)[0]

    arrived = swap(half_out(1, BF))
    (summed,) = call(core_sum, [((chips, rows, 2 * width), BF)], 0, 2)(half_out(0, F32), arrived)
    parts = exchange(summed)
    layer_out, tokens_grad = call(last_sum, [((rows, width), BF)] * 2, 0, 1)(parts)
    gate_g, up_g, down_g = call(
        weight_grads, [((ff, width), BF)] * 3, 0, 5, [pltpu.VMEM((total, wide), BF)], mib=12
    )(c0, c1, c2, c3, ordered)
    return (layer_out, tokens_grad, gate_g.T, up_g.T, down_g)


def solution(mesh):
    tok = P(GROUP, "col")
    wide = P("col", GROUP)

    def run(*args):
        return shards(mesh, *args)

    return jax.shard_map(
        run,
        mesh=mesh,
        in_specs=(tok, tok, wide, wide, tok),
        out_specs=(tok, tok, wide, wide, tok),
        check_vma=False,
    )
```

```python
import functools
import math

import jax
import jax.numpy as jnp
from jax import lax
from jax.experimental import pallas as pl
from jax.experimental.pallas import tpu as pltpu
from jax.sharding import PartitionSpec as P

BF = jnp.bfloat16
F32 = jnp.float32
GROUP = ("row", "depth")
NEAR = (0, -1, 1, 2)
ORDER = [(peer, step) for peer in range(4) for step in range(4)]


def nt(left, right):
    return lax.dot_general(left, right, (((1,), (1,)), ((), ())), preferred_element_type=F32)


def nn(left, right):
    return lax.dot_general(left, right, (((1,), (0,)), ((), ())), preferred_element_type=F32)


def tn(left, right):
    return lax.dot_general(left, right, (((0,), (0,)), ((), ())), preferred_element_type=F32)


def call(body, out_shapes, n_scalar, n_array, scratch=(), mib=8, outside=(), outside_out=()):
    def place(at, away):
        return pl.BlockSpec(memory_space=pltpu.HBM if at in away else pltpu.VMEM)

    return pl.pallas_call(
        body,
        out_shape=[jax.ShapeDtypeStruct(s, d) for s, d in out_shapes],
        in_specs=[pl.BlockSpec(memory_space=pltpu.SMEM)] * n_scalar
        + [place(at, outside) for at in range(n_array)],
        out_specs=[place(at, outside_out) for at in range(len(out_shapes))],
        scratch_shapes=list(scratch),
        compiler_params=pltpu.CompilerParams(vmem_limit_bytes=mib * 1024 * 1024),
    )


def coded(x):
    return (x * jnp.abs(x)).astype(BF)


def decoded(x):
    wide = x.astype(F32)
    return wide * lax.rsqrt(jnp.abs(wide) + 1e-36)


def spread(both, out):
    for at in range(out.shape[0]):
        out[at] = both[...]


def gather_rows(index, mine, other, ordered, slots):
    rows = mine.shape[1]
    for at, slot in enumerate(slots):
        ordered[2 * at * rows : (2 * at + 1) * rows, :] = mine[index[slot]]
        ordered[(2 * at + 1) * rows : (2 * at + 2) * rows, :] = other[index[slot]]


def partial_sums(index, mine, other, pair, down, third, first, second, own, kept, ordered, sems):
    width = pair.shape[1]
    both = pair.shape[0]
    block = own.shape[0]
    gather_rows(index, mine, other, ordered, range(16))
    copy = pltpu.make_async_copy(ordered, kept, sems.at[0])
    copy.start()
    gate_up = nt(ordered[:, :width], pair[...])
    cot = nt(ordered[:, width:], down[...])
    own[:, :both] = gate_up[:block, :]
    own[:, both:] = cot[:block, :]
    for at, out in ((3, third), (1, first), (2, second)):
        rows = slice(at * block, (at + 1) * block)
        out[:, :both] = coded(gate_up[rows, :])
        out[:, both:] = coded(cot[rows, :])
    copy.wait()


def near_sum(own, third, first, second, far, near, back, keep):
    chunk = keep.shape[0]

    def total(at):
        rows = slice(at * chunk, (at + 1) * chunk)
        return own[rows, :] + (decoded(first[rows, :]) + decoded(second[rows, :]) + decoded(third[rows, :]))

    far[...] = coded(total(2))
    near[...] = coded(total(1))
    back[...] = coded(total(3))
    keep[...] = total(0)


def swish(keep, far, near, back, out):
    ff = out.shape[1] // 3
    total = keep[...] + (decoded(near[...]) + decoded(far[...]) + decoded(back[...]))
    gate_sum = total[:, :ff]
    up_sum = total[:, ff : 2 * ff]
    hidden_cot = total[:, 2 * ff :]
    sig = jax.nn.sigmoid(gate_sum)
    gate_cot = hidden_cot * up_sum * sig * (1.0 + gate_sum * (1.0 - sig))
    up_cot = hidden_cot * gate_sum * sig
    out[:, :ff] = gate_cot.astype(BF)
    out[:, ff : 2 * ff] = up_cot.astype(BF)
    out[:, 2 * ff :] = (gate_sum * sig * up_sum).astype(BF)


def outward(half, index, c3, c1, c2, c0, pair, down, out, picked):
    width = pair.shape[1]
    both = pair.shape[0]
    rows = out.shape[1]
    for at, c in ((3, c3), (1, c1), (2, c2), (0, c0)):
        for j in range(4):
            slot = at * 4 + j
            first = j * 2 * rows + half * rows
            picked[slot * rows : (slot + 1) * rows, :] = c[first : first + rows, :]
    layer = nn(picked[:, both:], down[...]).astype(out.dtype)
    back = nn(picked[:, :both], pair[...]).astype(out.dtype)
    for slot in range(16):
        out[index[slot], :, :width] = layer[slot * rows : (slot + 1) * rows, :]
        out[index[slot], :, width:] = back[slot * rows : (slot + 1) * rows, :]


def core_sum(keep, arrived, out):
    out[...] = (keep[...] + arrived[...].astype(F32)).astype(BF)


def weight_grads(place, c0, c1, c2, c3, ordered, gate_g, up_g, down_g, allc):
    ff, width = gate_g.shape
    chunk = c0.shape[0] // 4
    scale = 1.0 / math.sqrt(ordered.shape[0])
    for at, c in enumerate((c0, c1, c2, c3)):
        for slot in [i for i, (peer, _) in enumerate(ORDER) if peer == at]:
            rows = pl.ds(pl.multiple_of(place[slot] * chunk, chunk), chunk)
            allc[slot * chunk : (slot + 1) * chunk, :] = c[rows, :]
    both = tn(allc[:, : 2 * ff], ordered[:, :width]) * scale
    gate_g[...] = both[:ff, :].astype(BF)
    up_g[...] = both[ff:, :].astype(BF)
    down_g[...] = (tn(allc[:, 2 * ff :], ordered[:, width:]) * scale).astype(BF)


def last_sum(parts, layer_out, tokens_grad):
    width = layer_out.shape[1]
    total = parts[0].astype(F32)
    for at in range(1, parts.shape[0]):
        total = total + parts[at].astype(F32)
    layer_out[...] = total[:, :width].astype(BF)
    tokens_grad[...] = total[:, width:].astype(BF)


def shards(mesh, tokens, cotangent, gate_weight, up_weight, down_weight):
    cols, depth = mesh.shape["col"], mesh.shape["depth"]
    ranks = mesh.shape["row"] * depth
    ff, width = down_weight.shape
    rows = tokens.shape[0]
    total = rows * ranks
    chunk = total // cols
    block = 4 * chunk
    wide = 3 * ff

    def shift(x, step):
        pairs = []
        for z in range(cols):
            for d in range(depth):
                to = (z + (step if d % 2 == 0 else -step)) % cols
                pairs.append((z * depth + d, to * depth + d))
        return lax.ppermute(x, ("col", "depth"), pairs)

    z = lax.axis_index("col")
    sign = 1 - 2 * (lax.axis_index("depth") % 2)
    peer_of = jnp.array([NEAR[peer] for peer, _ in ORDER], jnp.int32)
    step_of = jnp.array([step for _, step in ORDER], jnp.int32)
    peers = (z - sign * peer_of + 16) % 16
    place = (peers // 4 + sign * step_of + 4) % 4
    index = 4 * place + peers % 4
    row_of = jnp.array([at % 4 for at in range(16)], jnp.int32)
    near_of = jnp.array([NEAR[at // 4] for at in range(16)], jnp.int32)
    by_row = 4 * row_of + (z - sign * near_of + 16) % 4

    cores = 2
    chips = ranks // cores
    same_core = [[c + cores * a for a in range(chips)] for c in range(cores)]

    def swap(x):
        return lax.ppermute(x, "depth", [(d, d ^ 1) for d in range(depth)])

    def exchange(x):
        return lax.all_to_all(x, GROUP, 0, 0, tiled=True, axis_index_groups=same_core)

    both = jnp.concatenate([tokens, cotangent], axis=1)
    (sent,) = call(spread, [((chips, rows, 2 * width), BF)], 0, 1)(both)
    mine = exchange(sent)
    other = swap(mine)
    pair = jnp.concatenate([gate_weight.T, up_weight.T], axis=0)
    third, first, second, own, ordered = call(
        partial_sums,
        [((block, wide), BF)] * 3 + [((block, wide), F32), ((total, 2 * width), BF)],
        1,
        4,
        [pltpu.VMEM((total, 2 * width), BF), pltpu.SemaphoreType.DMA((1,))],
        mib=16,
        outside_out=(4,),
    )(index, mine, other, pair, down_weight)
    third = shift(third, -NEAR[3])
    first = shift(first, -NEAR[1])
    second = shift(second, -NEAR[2])
    far, near, back, keep = call(
        near_sum, [((chunk, wide), BF)] * 3 + [((chunk, wide), F32)], 0, 4
    )(own, third, first, second)
    far = shift(far, 8)
    near = shift(near, 4)
    back = shift(back, -4)
    (act,) = call(swish, [((chunk, wide), BF)], 0, 4)(keep, far, near, back)
    strided = [[i + 4 * j for j in range(4)] for i in range(4)]
    c0 = lax.all_gather(act, "col", axis=0, tiled=True, axis_index_groups=strided)
    c3 = shift(c0, NEAR[3])
    c1 = shift(c0, NEAR[1])
    c2 = shift(c0, NEAR[2])
    def half_out(half, dtype):
        return call(
            functools.partial(outward, half),
            [((chips, rows, 2 * width), dtype)],
            1,
            6,
            [pltpu.VMEM((total // cores, wide), BF)],
        )(by_row, c3, c1, c2, c0, pair, down_weight)[0]

    arrived = swap(half_out(1, BF))
    (summed,) = call(core_sum, [((chips, rows, 2 * width), BF)], 0, 2)(half_out(0, F32), arrived)
    parts = exchange(summed)
    layer_out, tokens_grad = call(last_sum, [((rows, width), BF)] * 2, 0, 1)(parts)
    gate_g, up_g, down_g = call(
        weight_grads, [((ff, width), BF)] * 3, 1, 5, [pltpu.VMEM((total, wide), BF)], mib=12
    )(place, c0, c1, c2, c3, ordered)
    return (layer_out, tokens_grad, gate_g.T, up_g.T, down_g)


def solution(mesh):
    tok = P(GROUP, "col")
    wide = P("col", GROUP)

    def run(*args):
        return shards(mesh, *args)

    return jax.shard_map(
        run,
        mesh=mesh,
        in_specs=(tok, tok, wide, wide, tok),
        out_specs=(tok, tok, wide, wide, tok),
        check_vma=False,
    )
```

```python
import functools
import math

import jax
import jax.numpy as jnp
from jax import lax
from jax.experimental import pallas as pl
from jax.experimental.pallas import tpu as pltpu
from jax.sharding import PartitionSpec as P

BF = jnp.bfloat16
F32 = jnp.float32
GROUP = ("row", "depth")
NEAR = (0, -1, 1, 2)


def peer(at):
    z = lax.axis_index("col")
    sign = 1 - 2 * lax.rem(lax.axis_index("depth"), 2)
    return lax.rem(z - sign * NEAR[at] + 16, 16), sign


def place(at, step):
    z, sign = peer(at)
    return lax.rem(z // 4 + sign * step + 4, 4)


def chunk_of(at, place_of):
    return 4 * place_of + lax.rem(peer(at)[0], 4)


def nt(left, right):
    return lax.dot_general(left, right, (((1,), (1,)), ((), ())), preferred_element_type=F32)


def nn(left, right):
    return lax.dot_general(left, right, (((1,), (0,)), ((), ())), preferred_element_type=F32)


def tn(left, right):
    return lax.dot_general(left, right, (((0,), (0,)), ((), ())), preferred_element_type=F32)


def call(body, out_shapes, n_scalar, n_array, scratch=(), mib=4, outside=(), outside_out=()):
    def place(at, away):
        return pl.BlockSpec(memory_space=pltpu.HBM if at in away else pltpu.VMEM)

    return pl.pallas_call(
        body,
        out_shape=[jax.ShapeDtypeStruct(s, d) for s, d in out_shapes],
        in_specs=[pl.BlockSpec(memory_space=pltpu.SMEM)] * n_scalar
        + [place(at, outside) for at in range(n_array)],
        out_specs=[place(at, outside_out) for at in range(len(out_shapes))],
        scratch_shapes=list(scratch),
        compiler_params=pltpu.CompilerParams(vmem_limit_bytes=mib * 1024 * 1024),
    )


def coded(x):
    return (x * jnp.abs(x)).astype(BF)


def decoded(x):
    wide = x.astype(F32)
    return wide * lax.rsqrt(jnp.abs(wide) + 1e-36)


def spread(both, out):
    for at in range(out.shape[0]):
        out[at] = both[...]


def stack(gate, gate_away, up, up_away, down, down_away, pair, both_down):
    ff = gate.shape[0]
    for at, rows in enumerate((gate, gate_away, up, up_away)):
        pair[at * ff : (at + 1) * ff, :] = rows[...]
    both_down[:ff, :] = down[...]
    both_down[ff:, :] = down_away[...]


def partial_sums(
    mine, w0, w1, w2, w3, w4, w5, third, first, second, own, kept, kept_pair, kept_down, ordered, pair, down, sems
):
    both, width = pair.shape
    block = own.shape[0]
    rows = mine.shape[1]
    for at in range(4):
        for step in range(4):
            to = at * block + step * rows
            ordered[to : to + rows, :] = mine[chunk_of(at, place(at, step))]
    stack(w0, w1, w2, w3, w4, w5, pair, down)
    copies = [
        pltpu.make_async_copy(held, to, sems.at[at])
        for at, (held, to) in enumerate(((ordered, kept), (pair, kept_pair), (down, kept_down)))
    ]
    for copy in copies:
        copy.start()
    gate_up = nt(ordered[:, :width], pair[...])
    cot = nt(ordered[:, width:], down[...])
    own[:, :both] = gate_up[:block, :]
    own[:, both:] = cot[:block, :]
    for at, out in ((3, third), (1, first), (2, second)):
        here = slice(at * block, (at + 1) * block)
        out[:, :both] = coded(gate_up[here, :])
        out[:, both:] = coded(cot[here, :])
    for copy in copies:
        copy.wait()


def near_sum(own, third, first, second, far, near, back, keep):
    chunk = keep.shape[0]

    def total(at):
        rows = slice(at * chunk, (at + 1) * chunk)
        return own[rows, :] + (decoded(first[rows, :]) + decoded(second[rows, :]) + decoded(third[rows, :]))

    far[...] = coded(total(2))
    near[...] = coded(total(1))
    back[...] = coded(total(3))
    keep[...] = total(0)


def swish(keep, far, near, back, out):
    ff = out.shape[1] // 3
    total = keep[...] + (decoded(near[...]) + decoded(far[...]) + decoded(back[...]))
    gate_sum = total[:, :ff]
    up_sum = total[:, ff : 2 * ff]
    hidden_cot = total[:, 2 * ff :]
    sig = jax.nn.sigmoid(gate_sum)
    gate_cot = hidden_cot * up_sum * sig * (1.0 + gate_sum * (1.0 - sig))
    up_cot = hidden_cot * gate_sum * sig
    out[:, :ff] = gate_cot.astype(BF)
    out[:, ff : 2 * ff] = up_cot.astype(BF)
    out[:, 2 * ff :] = (gate_sum * sig * up_sum).astype(BF)


def outward(c3, c1, c2, c0, pair, down, out, rows_of):
    both, width = pair.shape
    rows = out.shape[1]
    block = c0.shape[0]
    for at, c in ((3, c3), (1, c1), (2, c2), (0, c0)):
        rows_of[at * block : (at + 1) * block, :] = c[...]
    layer = nn(rows_of[:, both:], down[...]).astype(BF)
    back = nn(rows_of[:, :both], pair[...]).astype(BF)
    for at in range(4):
        for j in range(4):
            here = slice(at * block + j * rows, at * block + (j + 1) * rows)
            chunk = chunk_of(at, j)
            out[chunk, :, :width] = layer[here, :]
            out[chunk, :, width:] = back[here, :]


def weight_part(start, kind, c0, c1, c2, c3, ordered, part):
    width = ordered.shape[1] // 2
    size = part.shape[1]
    rows = c0.shape[0] // 4
    for at, c in enumerate((c0, c1, c2, c3)):
        for step in range(4):
            here = pl.ds(pl.multiple_of(place(at, step) * rows, rows), rows)
            to = at * c.shape[0] + step * rows
            part[to : to + rows, :] = c[here, start : start + size]
    tokens = ordered[:, width:] if kind == 2 else ordered[:, :width]
    return tn(part[...], tokens)


def weight_away(c0, c1, c2, c3, ordered, gate, up, down, part):
    ff = gate.shape[0]
    extra = part.shape[1] - ff
    for kind, out in enumerate((gate, up, down)):
        start = (2 * kind + 1) * ff - extra
        out[...] = coded(weight_part(start, kind, c0, c1, c2, c3, ordered, part)[extra:, :])


def weight_own(scale, c0, c1, c2, c3, ordered, a0, a1, a2, gate, up, down, part):
    ff = gate.shape[0]
    for kind, (arrived, out) in enumerate(((a0, gate), (a1, up), (a2, down))):
        sums = weight_part(2 * kind * ff, kind, c0, c1, c2, c3, ordered, part)[:ff, :]
        out[...] = ((sums + decoded(arrived[...])) * scale).astype(BF)


def last_sum(parts, layer_out, tokens_grad):
    width = layer_out.shape[1]
    total = parts[0].astype(F32)
    for at in range(1, parts.shape[0]):
        total = total + parts[at].astype(F32)
    layer_out[...] = total[:, :width].astype(BF)
    tokens_grad[...] = total[:, width:].astype(BF)


def shards(mesh, tokens, cotangent, gate_weight, up_weight, down_weight):
    cols, depth = mesh.shape["col"], mesh.shape["depth"]
    ranks = mesh.shape["row"] * depth
    ff, width = down_weight.shape
    rows = tokens.shape[0]
    total = rows * ranks
    cores = 2
    chips = ranks // cores
    chunk = rows
    block = 4 * chunk
    wide = 3 * cores * ff

    def shift(x, step):
        pairs = []
        for z in range(cols):
            for d in range(depth):
                to = (z + (step if d % 2 == 0 else -step)) % cols
                pairs.append((z * depth + d, to * depth + d))
        return lax.ppermute(x, ("col", "depth"), pairs)

    same_core = [[c + cores * a for a in range(chips)] for c in range(cores)]

    def swap(x):
        return lax.ppermute(x, "depth", [(d, d ^ 1) for d in range(depth)])

    def exchange(x):
        return lax.all_to_all(x, GROUP, 0, 0, tiled=True, axis_index_groups=same_core)

    both = jnp.concatenate([tokens, cotangent], axis=1)
    (sent,) = call(spread, [((chips, rows, 2 * width), BF)], 0, 1)(both)
    mine = exchange(sent)
    weights = []
    for held in (gate_weight.T, up_weight.T, down_weight):
        weights += [held, swap(held)]
    kept = [(4 * block, 2 * width), (4 * ff, width), (2 * ff, width)]
    third, first, second, own, ordered, pair, down = call(
        partial_sums,
        [((block, wide), BF)] * 3 + [((block, wide), F32)] + [(shape, BF) for shape in kept],
        0,
        7,
        [pltpu.VMEM(shape, BF) for shape in kept] + [pltpu.SemaphoreType.DMA((3,))],
        mib=10,
        outside_out=(4, 5, 6),
    )(mine, *weights)
    third = shift(third, -NEAR[3])
    first = shift(first, -NEAR[1])
    second = shift(second, -NEAR[2])
    far, near, back, keep = call(
        near_sum, [((chunk, wide), BF)] * 3 + [((chunk, wide), F32)], 0, 4
    )(own, third, first, second)
    far = shift(far, 8)
    near = shift(near, 4)
    back = shift(back, -4)
    (act,) = call(swish, [((chunk, wide), BF)], 0, 4)(keep, far, near, back)
    strided = [[i + 4 * j for j in range(4)] for i in range(4)]
    c0 = lax.all_gather(act, "col", axis=0, tiled=True, axis_index_groups=strided)
    c3 = shift(c0, NEAR[3])
    c1 = shift(c0, NEAR[1])
    c2 = shift(c0, NEAR[2])
    (out,) = call(
        outward,
        [((chips, rows, 2 * width), BF)],
        0,
        6,
        [pltpu.VMEM((4 * block, wide), BF)],
        mib=8,
    )(c3, c1, c2, c0, pair, down)
    out, c0, c1, c2, c3 = lax.optimization_barrier((out, c0, c1, c2, c3))
    parts = exchange(out)
    window = [pltpu.VMEM((4 * block, -(-ff // 128) * 128), BF)]
    grads = [((ff, width), BF)] * 3
    away = call(weight_away, grads, 0, 5, window, mib=8)(c0, c1, c2, c3, ordered)
    gate_g, up_g, down_g = call(
        functools.partial(weight_own, 1.0 / math.sqrt(total)), grads, 0, 8, window, mib=8
    )(c0, c1, c2, c3, ordered, *[swap(x) for x in away])
    parts, gate_g = lax.optimization_barrier((parts, gate_g))
    layer_out, tokens_grad = call(last_sum, [((rows, width), BF)] * 2, 0, 1)(parts)
    return (layer_out, tokens_grad, gate_g.T, up_g.T, down_g)


def solution(mesh):
    tok = P(GROUP, "col")
    wide = P("col", GROUP)

    def run(*args):
        return shards(mesh, *args)

    return jax.shard_map(
        run,
        mesh=mesh,
        in_specs=(tok, tok, wide, wide, tok),
        out_specs=(tok, tok, wide, wide, tok),
        check_vma=False,
    )
```

```python
import functools
import math

import jax
import jax.numpy as jnp
from jax import lax
from jax.experimental import pallas as pl
from jax.experimental.pallas import tpu as pltpu
from jax.sharding import PartitionSpec as P

BF = jnp.bfloat16
F32 = jnp.float32
GROUP = ("row", "depth")
NEAR = (0, -1, 1, 2)


def peer(at):
    z = lax.axis_index("col")
    sign = 1 - 2 * lax.rem(lax.axis_index("depth"), 2)
    return lax.rem(z - sign * NEAR[at] + 16, 16), sign


def place(at, step):
    z, sign = peer(at)
    return lax.rem(z // 4 + sign * step + 4, 4)


def chunk_of(at, place_of):
    return 4 * place_of + lax.rem(peer(at)[0], 4)


def nt(left, right):
    return lax.dot_general(left, right, (((1,), (1,)), ((), ())), preferred_element_type=F32)


def nn(left, right):
    return lax.dot_general(left, right, (((1,), (0,)), ((), ())), preferred_element_type=F32)


def tn(left, right):
    return lax.dot_general(left, right, (((0,), (0,)), ((), ())), preferred_element_type=F32)


def call(body, out_shapes, n_scalar, n_array, scratch=(), mib=4, outside=(), outside_out=()):
    def place(at, away):
        return pl.BlockSpec(memory_space=pltpu.HBM if at in away else pltpu.VMEM)

    return pl.pallas_call(
        body,
        out_shape=[jax.ShapeDtypeStruct(s, d) for s, d in out_shapes],
        in_specs=[pl.BlockSpec(memory_space=pltpu.SMEM)] * n_scalar
        + [place(at, outside) for at in range(n_array)],
        out_specs=[place(at, outside_out) for at in range(len(out_shapes))],
        scratch_shapes=list(scratch),
        compiler_params=pltpu.CompilerParams(vmem_limit_bytes=mib * 1024 * 1024),
    )


def coded(x):
    return (x * jnp.abs(x)).astype(BF)


def decoded(x):
    wide = x.astype(F32)
    return wide * lax.rsqrt(jnp.abs(wide) + 1e-36)


def spread(both, out):
    for at in range(out.shape[0]):
        out[at] = both[...]


def stack(gate, gate_away, up, up_away, down, down_away, pair, both_down):
    ff = gate.shape[0]
    for at, rows in enumerate((gate, gate_away, up, up_away)):
        pair[at * ff : (at + 1) * ff, :] = rows[...]
    both_down[:ff, :] = down[...]
    both_down[ff:, :] = down_away[...]


def partial_sums(mine, pair, down, third, first, second, own, kept, kept_pair, kept_down, ordered, sems):
    both, width = pair.shape
    block = own.shape[0]
    rows = mine.shape[1]
    for at in range(4):
        for step in range(4):
            to = at * block + step * rows
            ordered[to : to + rows, :] = mine[chunk_of(at, place(at, step))]
    copies = [
        pltpu.make_async_copy(held, to, sems.at[at])
        for at, (held, to) in enumerate(((ordered, kept), (pair, kept_pair), (down, kept_down)))
    ]
    for copy in copies:
        copy.start()
    gate_up = nt(ordered[:, :width], pair[...])
    cot = nt(ordered[:, width:], down[...])
    own[:, :both] = gate_up[:block, :]
    own[:, both:] = cot[:block, :]
    for at, out in ((3, third), (1, first), (2, second)):
        here = slice(at * block, (at + 1) * block)
        out[:, :both] = coded(gate_up[here, :])
        out[:, both:] = coded(cot[here, :])
    for copy in copies:
        copy.wait()


def near_sum(own, first, second, third, far, near, back, keep):
    chunk = keep.shape[0]

    def total(at):
        rows = slice(at * chunk, (at + 1) * chunk)
        return own[rows, :] + (decoded(first[rows, :]) + decoded(second[rows, :]) + decoded(third[rows, :]))

    far[...] = coded(total(2))
    near[...] = coded(total(1))
    back[...] = coded(total(3))
    keep[...] = total(0)


def swish(keep, far, near, back, out):
    ff = out.shape[1] // 3
    total = keep[...] + (decoded(near[...]) + decoded(far[...]) + decoded(back[...]))
    gate_sum = total[:, :ff]
    up_sum = total[:, ff : 2 * ff]
    hidden_cot = total[:, 2 * ff :]
    sig = jax.nn.sigmoid(gate_sum)
    gate_cot = hidden_cot * up_sum * sig * (1.0 + gate_sum * (1.0 - sig))
    up_cot = hidden_cot * gate_sum * sig
    out[:, :ff] = gate_cot.astype(BF)
    out[:, ff : 2 * ff] = up_cot.astype(BF)
    out[:, 2 * ff :] = (gate_sum * sig * up_sum).astype(BF)


def outward(c2, c1, c3, c0, pair, down, out, rows_of):
    both, width = pair.shape
    rows = out.shape[1]
    block = c0.shape[0]
    for at, c in ((2, c2), (1, c1), (3, c3), (0, c0)):
        rows_of[at * block : (at + 1) * block, :] = c[...]
    layer = nn(rows_of[:, both:], down[...]).astype(BF)
    back = nn(rows_of[:, :both], pair[...]).astype(BF)
    for at in range(4):
        for j in range(4):
            here = slice(at * block + j * rows, at * block + (j + 1) * rows)
            chunk = chunk_of(at, j)
            out[chunk, :, :width] = layer[here, :]
            out[chunk, :, width:] = back[here, :]


def weight_part(start, kind, c0, c1, c2, c3, ordered, part):
    width = ordered.shape[1] // 2
    size = part.shape[1]
    rows = c0.shape[0] // 4
    for at, c in enumerate((c0, c1, c2, c3)):
        for step in range(4):
            here = pl.ds(pl.multiple_of(place(at, step) * rows, rows), rows)
            to = at * c.shape[0] + step * rows
            part[to : to + rows, :] = c[here, start : start + size]
    tokens = ordered[:, width:] if kind == 2 else ordered[:, :width]
    return tn(part[...], tokens)


def weight_away(c0, c1, c2, c3, ordered, gate, up, down, part):
    ff = gate.shape[0]
    extra = part.shape[1] - ff
    for kind, out in enumerate((gate, up, down)):
        start = (2 * kind + 1) * ff - extra
        out[...] = coded(weight_part(start, kind, c0, c1, c2, c3, ordered, part)[extra:, :])


def weight_own(scale, c0, c1, c2, c3, ordered, a0, a1, a2, gate, up, down, part):
    ff = gate.shape[0]
    for kind, (arrived, out) in enumerate(((a0, gate), (a1, up), (a2, down))):
        sums = weight_part(2 * kind * ff, kind, c0, c1, c2, c3, ordered, part)[:ff, :]
        out[...] = ((sums + decoded(arrived[...])) * scale).astype(BF)


def last_sum(parts, layer_out, tokens_grad):
    width = layer_out.shape[1]
    total = parts[0].astype(F32)
    for at in range(1, parts.shape[0]):
        total = total + parts[at].astype(F32)
    layer_out[...] = total[:, :width].astype(BF)
    tokens_grad[...] = total[:, width:].astype(BF)


def shards(mesh, tokens, cotangent, gate_weight, up_weight, down_weight):
    cols, depth = mesh.shape["col"], mesh.shape["depth"]
    ranks = mesh.shape["row"] * depth
    ff, width = down_weight.shape
    rows = tokens.shape[0]
    total = rows * ranks
    cores = 2
    chips = ranks // cores
    chunk = rows
    block = 4 * chunk
    wide = 3 * cores * ff

    def shift(x, step):
        pairs = []
        for z in range(cols):
            for d in range(depth):
                to = (z + (step if d % 2 == 0 else -step)) % cols
                pairs.append((z * depth + d, to * depth + d))
        return lax.ppermute(x, ("col", "depth"), pairs)

    same_core = [[c + cores * a for a in range(chips)] for c in range(cores)]

    def swap(x):
        return lax.ppermute(x, "depth", [(d, d ^ 1) for d in range(depth)])

    def exchange(x):
        return lax.all_to_all(x, GROUP, 0, 0, tiled=True, axis_index_groups=same_core)

    both = jnp.concatenate([tokens, cotangent], axis=1)
    (sent,) = call(spread, [((chips, rows, 2 * width), BF)], 0, 1)(both)
    mine = exchange(sent)
    weights = []
    for held in (gate_weight.T, up_weight.T, down_weight):
        weights += [held, swap(held)]
    kept = [(4 * block, 2 * width), (4 * ff, width), (2 * ff, width)]
    third, first, second, own, ordered, pair, down = call(
        partial_sums,
        [((block, wide), BF)] * 3 + [((block, wide), F32)] + [(shape, BF) for shape in kept],
        0,
        3,
        [pltpu.VMEM(kept[0], BF), pltpu.SemaphoreType.DMA((3,))],
        mib=10,
        outside_out=(4, 5, 6),
    )(mine, *call(stack, [(shape, BF) for shape in kept[1:]], 0, 6, mib=4)(*weights))
    third = shift(third, -NEAR[3])
    first = shift(first, -NEAR[1])
    second = shift(second, -NEAR[2])
    far, near, back, keep = call(
        near_sum, [((chunk, wide), BF)] * 3 + [((chunk, wide), F32)], 0, 4
    )(own, first, second, third)
    far = shift(far, 8)
    near = shift(near, 4)
    back = shift(back, -4)
    (act,) = call(swish, [((chunk, wide), BF)], 0, 4)(keep, far, near, back)
    strided = [[i + 4 * j for j in range(4)] for i in range(4)]
    c0 = lax.all_gather(act, "col", axis=0, tiled=True, axis_index_groups=strided)
    c3 = shift(c0, NEAR[3])
    c1 = shift(c0, NEAR[1])
    c2 = shift(c0, NEAR[2])
    (out,) = call(
        outward,
        [((chips, rows, 2 * width), BF)],
        0,
        6,
        [pltpu.VMEM((4 * block, wide), BF)],
        mib=8,
    )(c2, c1, c3, c0, pair, down)
    out, c0, c1, c2, c3 = lax.optimization_barrier((out, c0, c1, c2, c3))
    parts = exchange(out)
    window = [pltpu.VMEM((4 * block, -(-ff // 128) * 128), BF)]
    grads = [((ff, width), BF)] * 3
    away = call(weight_away, grads, 0, 5, window, mib=8)(c0, c1, c2, c3, ordered)
    gate_g, up_g, down_g = call(
        functools.partial(weight_own, 1.0 / math.sqrt(total)), grads, 0, 8, window, mib=8
    )(c0, c1, c2, c3, ordered, *[swap(x) for x in away])
    parts, gate_g = lax.optimization_barrier((parts, gate_g))
    layer_out, tokens_grad = call(last_sum, [((rows, width), BF)] * 2, 0, 1)(parts)
    return (layer_out, tokens_grad, gate_g.T, up_g.T, down_g)


def solution(mesh):
    tok = P(GROUP, "col")
    wide = P("col", GROUP)

    def run(*args):
        return shards(mesh, *args)

    return jax.shard_map(
        run,
        mesh=mesh,
        in_specs=(tok, tok, wide, wide, tok),
        out_specs=(tok, tok, wide, wide, tok),
        check_vma=False,
    )
```

```python
import functools
import math

import jax
import jax.numpy as jnp
from jax import lax
from jax.experimental import pallas as pl
from jax.experimental.pallas import tpu as pltpu
from jax.sharding import PartitionSpec as P

BF = jnp.bfloat16
F32 = jnp.float32
GROUP = ("row", "depth")
NEAR = (0, -1, 1, 2)


def peer(at):
    z = lax.axis_index("col")
    sign = 1 - 2 * lax.rem(lax.axis_index("depth"), 2)
    return lax.rem(z - sign * NEAR[at] + 16, 16), sign


def place(at, step):
    z, sign = peer(at)
    return lax.rem(z // 4 + sign * step + 4, 4)


def chunk_of(at, place_of):
    return 4 * place_of + lax.rem(peer(at)[0], 4)


def nt(left, right):
    return lax.dot_general(left, right, (((1,), (1,)), ((), ())), preferred_element_type=F32)


def nn(left, right):
    return lax.dot_general(left, right, (((1,), (0,)), ((), ())), preferred_element_type=F32)


def tn(left, right):
    return lax.dot_general(left, right, (((0,), (0,)), ((), ())), preferred_element_type=F32)


def call(body, out_shapes, n_scalar, n_array, scratch=(), mib=4, outside=(), outside_out=()):
    def place(at, away):
        return pl.BlockSpec(memory_space=pltpu.HBM if at in away else pltpu.VMEM)

    return pl.pallas_call(
        body,
        out_shape=[jax.ShapeDtypeStruct(s, d) for s, d in out_shapes],
        in_specs=[pl.BlockSpec(memory_space=pltpu.SMEM)] * n_scalar
        + [place(at, outside) for at in range(n_array)],
        out_specs=[place(at, outside_out) for at in range(len(out_shapes))],
        scratch_shapes=list(scratch),
        compiler_params=pltpu.CompilerParams(vmem_limit_bytes=mib * 1024 * 1024),
    )


def coded(x):
    return (x * jnp.abs(x)).astype(BF)


def decoded(x):
    wide = x.astype(F32)
    return wide * lax.rsqrt(jnp.abs(wide) + 1e-36)


def spread(both, out):
    for at in range(out.shape[0]):
        out[at] = both[...]


def stack(gate, gate_away, up, up_away, down, down_away, pair, both_down):
    ff = gate.shape[0]
    for at, rows in enumerate((gate, gate_away, up, up_away)):
        pair[at * ff : (at + 1) * ff, :] = rows[...]
    both_down[:ff, :] = down[...]
    both_down[ff:, :] = down_away[...]


def partial_sums(mine, pair, down, third, first, second, own, kept, kept_pair, kept_down, ordered, sems):
    both, width = pair.shape
    block = own.shape[0]
    rows = mine.shape[1]
    for at in range(4):
        for step in range(4):
            to = at * block + step * rows
            ordered[to : to + rows, :] = mine[chunk_of(at, place(at, step))]
    copies = [
        pltpu.make_async_copy(held, to, sems.at[at])
        for at, (held, to) in enumerate(((ordered, kept), (pair, kept_pair), (down, kept_down)))
    ]
    for copy in copies:
        copy.start()
    gate_up = nt(ordered[:, :width], pair[...])
    cot = nt(ordered[:, width:], down[...])
    own[:, :both] = gate_up[:block, :]
    own[:, both:] = cot[:block, :]
    for at, out in ((3, third), (1, first), (2, second)):
        here = slice(at * block, (at + 1) * block)
        out[:, :both] = coded(gate_up[here, :])
        out[:, both:] = coded(cot[here, :])
    for copy in copies:
        copy.wait()


def near_sum(own, first, second, third, far, near, back, keep):
    chunk = keep.shape[0]

    def total(at):
        rows = slice(at * chunk, (at + 1) * chunk)
        return own[rows, :] + (decoded(first[rows, :]) + decoded(second[rows, :]) + decoded(third[rows, :]))

    far[...] = coded(total(2))
    near[...] = coded(total(1))
    back[...] = coded(total(3))
    keep[...] = total(0)


def swish(keep, far, near, back, out):
    ff = out.shape[1] // 3
    total = keep[...] + (decoded(near[...]) + decoded(far[...]) + decoded(back[...]))
    gate_sum = total[:, :ff]
    up_sum = total[:, ff : 2 * ff]
    hidden_cot = total[:, 2 * ff :]
    sig = jax.nn.sigmoid(gate_sum)
    gate_cot = hidden_cot * up_sum * sig * (1.0 + gate_sum * (1.0 - sig))
    up_cot = hidden_cot * gate_sum * sig
    out[:, :ff] = gate_cot.astype(BF)
    out[:, ff : 2 * ff] = up_cot.astype(BF)
    out[:, 2 * ff :] = (gate_sum * sig * up_sum).astype(BF)


def products(rows_of, pair, down, out):
    both, width = pair.shape
    out[:, :width] = nn(rows_of[:, both:], down[...]).astype(BF)
    out[:, width:] = nn(rows_of[:, :both], pair[...]).astype(BF)


def outward_early(c1, c3, c0, pair, down, out, rows_of):
    block = c0.shape[0]
    for slot, c in enumerate((c3, c1, c0)):
        rows_of[slot * block : (slot + 1) * block, :] = c[...]
    products(rows_of, pair, down, out)


def outward(c2, early, pair, down, out, last):
    rows = out.shape[1]
    block = c2.shape[0]
    for slot, at in enumerate((3, 1, 0)):
        for j in range(4):
            here = slot * block + j * rows
            out[chunk_of(at, j)] = early[here : here + rows, :]
    products(c2, pair, down, last)
    for j in range(4):
        out[chunk_of(2, j)] = last[j * rows : (j + 1) * rows, :]


def weight_part(start, kind, c0, c1, c2, c3, ordered, part):
    width = ordered.shape[1] // 2
    size = part.shape[1]
    rows = c0.shape[0] // 4
    for at, c in enumerate((c0, c1, c2, c3)):
        for step in range(4):
            here = pl.ds(pl.multiple_of(place(at, step) * rows, rows), rows)
            to = at * c.shape[0] + step * rows
            part[to : to + rows, :] = c[here, start : start + size]
    tokens = ordered[:, width:] if kind == 2 else ordered[:, :width]
    return tn(part[...], tokens)


def weight_away(c0, c1, c2, c3, ordered, gate, up, down, part):
    ff = gate.shape[0]
    extra = part.shape[1] - ff
    for kind, out in enumerate((gate, up, down)):
        start = (2 * kind + 1) * ff - extra
        out[...] = coded(weight_part(start, kind, c0, c1, c2, c3, ordered, part)[extra:, :])


def weight_own(scale, c0, c1, c2, c3, ordered, a0, a1, a2, gate, up, down, part):
    ff = gate.shape[0]
    for kind, (arrived, out) in enumerate(((a0, gate), (a1, up), (a2, down))):
        sums = weight_part(2 * kind * ff, kind, c0, c1, c2, c3, ordered, part)[:ff, :]
        out[...] = ((sums + decoded(arrived[...])) * scale).astype(BF)


def last_sum(parts, layer_out, tokens_grad):
    width = layer_out.shape[1]
    total = parts[0].astype(F32)
    for at in range(1, parts.shape[0]):
        total = total + parts[at].astype(F32)
    layer_out[...] = total[:, :width].astype(BF)
    tokens_grad[...] = total[:, width:].astype(BF)


def shards(mesh, tokens, cotangent, gate_weight, up_weight, down_weight):
    cols, depth = mesh.shape["col"], mesh.shape["depth"]
    ranks = mesh.shape["row"] * depth
    ff, width = down_weight.shape
    rows = tokens.shape[0]
    total = rows * ranks
    cores = 2
    chips = ranks // cores
    chunk = rows
    block = 4 * chunk
    wide = 3 * cores * ff

    def shift(x, step):
        pairs = []
        for z in range(cols):
            for d in range(depth):
                to = (z + (step if d % 2 == 0 else -step)) % cols
                pairs.append((z * depth + d, to * depth + d))
        return lax.ppermute(x, ("col", "depth"), pairs)

    same_core = [[c + cores * a for a in range(chips)] for c in range(cores)]

    def swap(x):
        return lax.ppermute(x, "depth", [(d, d ^ 1) for d in range(depth)])

    def exchange(x):
        return lax.all_to_all(x, GROUP, 0, 0, tiled=True, axis_index_groups=same_core)

    both = jnp.concatenate([tokens, cotangent], axis=1)
    (sent,) = call(spread, [((chips, rows, 2 * width), BF)], 0, 1)(both)
    mine = exchange(sent)
    weights = []
    for held in (gate_weight.T, up_weight.T, down_weight):
        weights += [held, swap(held)]
    kept = [(4 * block, 2 * width), (4 * ff, width), (2 * ff, width)]
    third, first, second, own, ordered, pair, down = call(
        partial_sums,
        [((block, wide), BF)] * 3 + [((block, wide), F32)] + [(shape, BF) for shape in kept],
        0,
        3,
        [pltpu.VMEM(kept[0], BF), pltpu.SemaphoreType.DMA((3,))],
        mib=10,
        outside_out=(4, 5, 6),
    )(mine, *call(stack, [(shape, BF) for shape in kept[1:]], 0, 6, mib=4)(*weights))
    third = shift(third, -NEAR[3])
    first = shift(first, -NEAR[1])
    second = shift(second, -NEAR[2])
    far, near, back, keep = call(
        near_sum, [((chunk, wide), BF)] * 3 + [((chunk, wide), F32)], 0, 4
    )(own, first, second, third)
    far = shift(far, 8)
    near = shift(near, 4)
    back = shift(back, -4)
    (act,) = call(swish, [((chunk, wide), BF)], 0, 4)(keep, far, near, back)
    strided = [[i + 4 * j for j in range(4)] for i in range(4)]
    c0 = lax.all_gather(act, "col", axis=0, tiled=True, axis_index_groups=strided)
    c3 = shift(c0, NEAR[3])
    c1 = shift(c0, NEAR[1])
    c2 = shift(c0, NEAR[2])
    (early,) = call(
        outward_early,
        [((3 * block, 2 * width), BF)],
        0,
        5,
        [pltpu.VMEM((3 * block, wide), BF)],
        mib=8,
    )(c1, c3, c0, pair, down)
    (out,) = call(
        outward,
        [((chips, rows, 2 * width), BF)],
        0,
        4,
        [pltpu.VMEM((block, 2 * width), BF)],
        mib=8,
    )(c2, early, pair, down)
    out, c0, c1, c2, c3 = lax.optimization_barrier((out, c0, c1, c2, c3))
    parts = exchange(out)
    window = [pltpu.VMEM((4 * block, -(-ff // 128) * 128), BF)]
    grads = [((ff, width), BF)] * 3
    away = call(weight_away, grads, 0, 5, window, mib=8)(c0, c1, c2, c3, ordered)
    gate_g, up_g, down_g = call(
        functools.partial(weight_own, 1.0 / math.sqrt(total)), grads, 0, 8, window, mib=8
    )(c0, c1, c2, c3, ordered, *[swap(x) for x in away])
    parts, gate_g = lax.optimization_barrier((parts, gate_g))
    layer_out, tokens_grad = call(last_sum, [((rows, width), BF)] * 2, 0, 1)(parts)
    return (layer_out, tokens_grad, gate_g.T, up_g.T, down_g)


def solution(mesh):
    tok = P(GROUP, "col")
    wide = P("col", GROUP)

    def run(*args):
        return shards(mesh, *args)

    return jax.shard_map(
        run,
        mesh=mesh,
        in_specs=(tok, tok, wide, wide, tok),
        out_specs=(tok, tok, wide, wide, tok),
        check_vma=False,
    )
```

```python
import functools
import math

import jax
import jax.numpy as jnp
from jax import lax
from jax.experimental import pallas as pl
from jax.experimental.pallas import tpu as pltpu
from jax.sharding import PartitionSpec as P

BF = jnp.bfloat16
F32 = jnp.float32
GROUP = ("row", "depth")
NEAR = (0, -1, 1, 2)


def peer(at):
    z = lax.axis_index("col")
    sign = 1 - 2 * lax.rem(lax.axis_index("depth"), 2)
    return lax.rem(z - sign * NEAR[at] + 16, 16), sign


def place(at, step):
    z, sign = peer(at)
    return lax.rem(z // 4 + sign * step + 4, 4)


def chunk_of(at, place_of):
    return 4 * place_of + lax.rem(peer(at)[0], 4)


def nt(left, right):
    return lax.dot_general(left, right, (((1,), (1,)), ((), ())), preferred_element_type=F32)


def nn(left, right):
    return lax.dot_general(left, right, (((1,), (0,)), ((), ())), preferred_element_type=F32)


def tn(left, right):
    return lax.dot_general(left, right, (((0,), (0,)), ((), ())), preferred_element_type=F32)


def call(body, out_shapes, n_scalar, n_array, scratch=(), mib=4, outside=(), outside_out=()):
    def place(at, away):
        return pl.BlockSpec(memory_space=pltpu.HBM if at in away else pltpu.VMEM)

    return pl.pallas_call(
        body,
        out_shape=[jax.ShapeDtypeStruct(s, d) for s, d in out_shapes],
        in_specs=[pl.BlockSpec(memory_space=pltpu.SMEM)] * n_scalar
        + [place(at, outside) for at in range(n_array)],
        out_specs=[place(at, outside_out) for at in range(len(out_shapes))],
        scratch_shapes=list(scratch),
        compiler_params=pltpu.CompilerParams(vmem_limit_bytes=mib * 1024 * 1024),
    )


def coded(x):
    return (x * jnp.abs(x)).astype(BF)


def decoded(x):
    wide = x.astype(F32)
    return wide * lax.rsqrt(jnp.abs(wide) + 1e-36)


def spread(both, out):
    for at in range(out.shape[0]):
        out[at] = both[...]


def stack(gate, gate_away, up, up_away, down, down_away, pair, both_down):
    ff = gate.shape[0]
    for at, rows in enumerate((gate, gate_away, up, up_away)):
        pair[at * ff : (at + 1) * ff, :] = rows[...]
    both_down[:ff, :] = down[...]
    both_down[ff:, :] = down_away[...]


def partial_sums(mine, pair, down, third, first, second, own, kept, kept_pair, kept_down, ordered, sems):
    both, width = pair.shape
    block = own.shape[0]
    rows = mine.shape[1]
    for at in range(4):
        for step in range(4):
            to = at * block + step * rows
            ordered[to : to + rows, :] = mine[chunk_of(at, place(at, step))]
    copies = [
        pltpu.make_async_copy(held, to, sems.at[at])
        for at, (held, to) in enumerate(((ordered, kept), (pair, kept_pair), (down, kept_down)))
    ]
    for copy in copies:
        copy.start()
    gate_up = nt(ordered[:, :width], pair[...])
    cot = nt(ordered[:, width:], down[...])
    own[:, :both] = gate_up[:block, :]
    own[:, both:] = cot[:block, :]
    for at, out in ((3, third), (1, first), (2, second)):
        here = slice(at * block, (at + 1) * block)
        out[:, :both] = coded(gate_up[here, :])
        out[:, both:] = coded(cot[here, :])
    for copy in copies:
        copy.wait()


def near_sum(own, first, second, third, far, near, back, keep):
    chunk = keep.shape[0]

    def total(at):
        rows = slice(at * chunk, (at + 1) * chunk)
        return own[rows, :] + (decoded(first[rows, :]) + decoded(second[rows, :]) + decoded(third[rows, :]))

    far[...] = coded(total(2))
    near[...] = coded(total(1))
    back[...] = coded(total(3))
    keep[...] = total(0)


def swish(keep, far, near, back, out):
    ff = out.shape[1] // 3
    total = keep[...] + (decoded(near[...]) + decoded(far[...]) + decoded(back[...]))
    gate_sum = total[:, :ff]
    up_sum = total[:, ff : 2 * ff]
    hidden_cot = total[:, 2 * ff :]
    sig = jax.nn.sigmoid(gate_sum)
    gate_cot = hidden_cot * up_sum * sig * (1.0 + gate_sum * (1.0 - sig))
    up_cot = hidden_cot * gate_sum * sig
    out[:, :ff] = gate_cot.astype(BF)
    out[:, ff : 2 * ff] = up_cot.astype(BF)
    out[:, 2 * ff :] = (gate_sum * sig * up_sum).astype(BF)


def products(rows_of, pair, down, out):
    both, width = pair.shape
    out[:, :width] = nn(rows_of[:, both:], down[...]).astype(BF)
    out[:, width:] = nn(rows_of[:, :both], pair[...]).astype(BF)


def outward_early(c1, c3, c0, pair, down, out, rows_of):
    block = c0.shape[0]
    for slot, c in enumerate((c3, c1, c0)):
        rows_of[slot * block : (slot + 1) * block, :] = c[...]
    products(rows_of, pair, down, out)


def outward(c2, early, pair, down, out, last):
    rows = out.shape[1]
    block = c2.shape[0]
    for slot, at in enumerate((3, 1, 0)):
        for j in range(4):
            here = slot * block + j * rows
            out[chunk_of(at, j)] = early[here : here + rows, :]
    products(c2, pair, down, last)
    for j in range(4):
        out[chunk_of(2, j)] = last[j * rows : (j + 1) * rows, :]


def weight_part(start, kind, c0, c1, c2, c3, ordered, part):
    width = ordered.shape[1] // 2
    size = part.shape[1]
    rows = c0.shape[0] // 4
    for at, c in enumerate((c0, c1, c2, c3)):
        for step in range(4):
            here = pl.ds(pl.multiple_of(place(at, step) * rows, rows), rows)
            to = at * c.shape[0] + step * rows
            part[to : to + rows, :] = c[here, start : start + size]
    tokens = ordered[:, width:] if kind == 2 else ordered[:, :width]
    return tn(part[...], tokens)


def weight_away(c0, c1, c2, c3, ordered, gate, up, down, part):
    ff = gate.shape[0]
    extra = part.shape[1] - ff
    for kind, out in enumerate((gate, up, down)):
        start = (2 * kind + 1) * ff - extra
        out[...] = coded(weight_part(start, kind, c0, c1, c2, c3, ordered, part)[extra:, :])


def weight_own(scale, c0, c1, c2, c3, ordered, a0, a1, a2, gate, up, down, part):
    ff = gate.shape[0]
    for kind, (arrived, out) in enumerate(((a0, gate), (a1, up), (a2, down))):
        sums = weight_part(2 * kind * ff, kind, c0, c1, c2, c3, ordered, part)[:ff, :]
        out[...] = ((sums + decoded(arrived[...])) * scale).astype(BF)


def last_sum(parts, layer_out, tokens_grad):
    width = layer_out.shape[1]
    total = parts[0].astype(F32)
    for at in range(1, parts.shape[0]):
        total = total + parts[at].astype(F32)
    layer_out[...] = total[:, :width].astype(BF)
    tokens_grad[...] = total[:, width:].astype(BF)


def shards(mesh, tokens, cotangent, gate_weight, up_weight, down_weight):
    cols, depth = mesh.shape["col"], mesh.shape["depth"]
    ranks = mesh.shape["row"] * depth
    ff, width = down_weight.shape
    rows = tokens.shape[0]
    total = rows * ranks
    cores = 2
    chips = ranks // cores
    chunk = rows
    block = 4 * chunk
    wide = 3 * cores * ff

    def shift(x, step):
        pairs = []
        for z in range(cols):
            for d in range(depth):
                to = (z + (step if d % 2 == 0 else -step)) % cols
                pairs.append((z * depth + d, to * depth + d))
        return lax.ppermute(x, ("col", "depth"), pairs)

    same_core = [[c + cores * a for a in range(chips)] for c in range(cores)]

    def swap(x):
        return lax.ppermute(x, "depth", [(d, d ^ 1) for d in range(depth)])

    def exchange(x):
        return lax.all_to_all(x, GROUP, 0, 0, tiled=True, axis_index_groups=same_core)

    both = jnp.concatenate([tokens, cotangent], axis=1)
    (sent,) = call(spread, [((chips, rows, 2 * width), BF)], 0, 1)(both)
    mine = exchange(sent)
    weights = []
    for held in (gate_weight.T, up_weight.T, down_weight):
        weights += [held, swap(held)]
    kept = [(4 * block, 2 * width), (4 * ff, width), (2 * ff, width)]
    third, first, second, own, ordered, pair, down = call(
        partial_sums,
        [((block, wide), BF)] * 3 + [((block, wide), F32)] + [(shape, BF) for shape in kept],
        0,
        3,
        [pltpu.VMEM(kept[0], BF), pltpu.SemaphoreType.DMA((3,))],
        mib=10,
        outside_out=(4, 5, 6),
    )(mine, *call(stack, [(shape, BF) for shape in kept[1:]], 0, 6, mib=4)(*weights))
    third = shift(third, -NEAR[3])
    first = shift(first, -NEAR[1])
    second = shift(second, -NEAR[2])
    far, near, back, keep = call(
        near_sum, [((chunk, wide), BF)] * 3 + [((chunk, wide), F32)], 0, 4
    )(own, first, second, third)
    far = shift(far, 8)
    near = shift(near, 4)
    back = shift(back, -4)
    (act,) = call(swish, [((chunk, wide), BF)], 0, 4)(keep, far, near, back)
    strided = [[i + 4 * j for j in range(4)] for i in range(4)]
    c0 = lax.all_gather(act, "col", axis=0, tiled=True, axis_index_groups=strided)
    c3 = shift(c0, NEAR[3])
    c1 = shift(c0, NEAR[1])
    c2 = shift(c0, NEAR[2])
    (early,) = call(
        outward_early,
        [((3 * block, 2 * width), BF)],
        0,
        5,
        [pltpu.VMEM((3 * block, wide), BF)],
        mib=8,
    )(c1, c3, c0, pair, down)
    (out,) = call(
        outward,
        [((chips, rows, 2 * width), BF)],
        0,
        4,
        [pltpu.VMEM((block, 2 * width), BF)],
        mib=8,
    )(c2, early, pair, down)
    out, c0, c1, c2, c3 = lax.optimization_barrier((out, c0, c1, c2, c3))
    parts = exchange(out)
    window = [pltpu.VMEM((4 * block, -(-ff // 128) * 128), BF)]
    grads = [((ff, width), BF)] * 3
    away = call(weight_away, grads, 0, 5, window, mib=8)(c0, c1, c2, c3, ordered)
    gate_g, up_g, down_g = call(
        functools.partial(weight_own, 1.0 / math.sqrt(total)), grads, 0, 8, window, mib=8
    )(c0, c1, c2, c3, ordered, *[swap(x) for x in away])
    layer_out, tokens_grad = call(last_sum, [((rows, width), BF)] * 2, 0, 1)(parts)
    return (layer_out, tokens_grad, gate_g.T, up_g.T, down_g)


def solution(mesh):
    tok = P(GROUP, "col")
    wide = P("col", GROUP)

    def run(*args):
        return shards(mesh, *args)

    return jax.shard_map(
        run,
        mesh=mesh,
        in_specs=(tok, tok, wide, wide, tok),
        out_specs=(tok, tok, wide, wide, tok),
        check_vma=False,
    )
```
